256 devices in a mesh: dap: 64 (over x, y_hi, z), rep: 4 (over y_lo, core).
Axes of the slice: x: 4, y: 4 (y_hi: 2, y_lo: 2; y = y_hi * 2 + y_lo), z: 8, core: 2. Of those that a mesh axis runs over, the one named last changes fastest.
Arguments:
- pair: bfloat16 [2048, 512, 128], P(('rep', 'dap')), parts along dimension 0, may hold values from -100 to 100
- pair_mask: int32 [2048, 512], P(('rep', 'dap')), parts along dimension 0, may hold values 0 or 1
- chain_ids: int32 [2048], P('rep'), parts along dimension 0, may hold values from 0 to 3, never falling along the last dimension, each value on 1 to 256 neighbouring positions
- norm_gain: float32 [3, 128], replicated, may hold values from 0.5 to 1.5
- norm_shift: float32 [3, 128], replicated, may hold values from -3 to 3
- attn_proj: bfloat16 [2, 128, 512], replicated, may hold values from -1 to 1
- gate_shift: float32 [2, 128], replicated, may hold values from -4 to 4
- bias_proj: bfloat16 [2, 128, 4], replicated, may hold values from -4 to 4
- chain_scale: float32 [2, 4], replicated, may hold values from -2 to 250
- attn_out: bfloat16 [2, 128, 128], replicated, may hold values from -0.5 to 0.5
- trans_in: bfloat16 [128, 512], replicated, may hold values from -0.5 to 0.5
- trans_out: bfloat16 [512, 128], replicated, may hold values from -0.25 to 0.25
Outputs:
- updated: bfloat16 [2048, 512, 128], P(('rep', 'dap')), parts along dimension 0
The draws below stay inside these ranges and needn't reach their ends.
There are 4 independent parts, one for each index of `rep`. The reference program is written for one: setup_inputs(seed, part) draws one part's arguments, and reference() takes and returns one part's arrays. A program takes and returns all parts, laid end to end along the dimension named above; an argument that names none is the same for every part. Nothing has to cross between parts.
Inputs may be any that keep to these rules, and one draw needn't show every extreme that they name: `chain_ids`: never falls along the residues.
All inputs are finite; a program needn't handle non-finite values. No bound on the sum of `pair_mask` on one device may be relied on, other than what follows from the above.
Results may differ from the reference program's by a relative error of at most 0.02.
Values may be sent and summed in bfloat16 or wider, within the bound.
A program may use at most 64 MiB of HBM per device.

```python
import math
import jax
import jax.numpy as jnp
import numpy as np
from jax import lax

C = 128
HEADS = 4
HEAD_DIM = 32
TRANS = 512
N_RES = 512


def draw_pair(key, part):
    key = jax.random.fold_in(key, 5)
    key_base = jax.random.fold_in(key, 0)
    base = jax.random.normal(key_base, (N_RES, N_RES, C), jnp.float32)
    return jnp.clip(base, -100.0, 100.0).astype(jnp.bfloat16)


def draw_bias_proj(key, part):
    key = jax.random.fold_in(key, 9)
    weights = jax.random.normal(key, (2, C, HEADS), jnp.float32) * C ** (-0.5)
    return jnp.clip(weights, -4.0, 4.0).astype(jnp.bfloat16)


def draw_chain_scale(key, part):
    key = jax.random.fold_in(key, 13)
    key_base = jax.random.fold_in(key, 0)
    values = jax.random.uniform(key_base, (2, HEADS), jnp.float32, -2.0, 2.0)
    return values


def set_ends(values, stream_key, smallest, largest):
    place = [jax.random.randint(jax.random.fold_in(stream_key, axis), (), 0, length) for axis, length in enumerate(values.shape)]
    widest = values.shape.index(max(values.shape))
    neighbour = place[:widest] + [(place[widest] + 1) % values.shape[widest]] + place[widest + 1:]
    return values.at[tuple(place)].set(smallest).at[tuple(neighbour)].set(largest)


def split_up(count, total, limit, lean):
    loads = [(1 << 20) // math.isqrt(grade ** lean) + 1 for grade in range(2, count + 1)]
    spare, holding = total - limit - (count - 1), [1] * (count - 1)
    while spare > 0:
        free = [i for i in range(count - 1) if holding[i] < limit]
        pool, remaining = sum([loads[i] for i in free]), spare
        for i in free:
            addition = min(limit - holding[i], max(1, remaining * loads[i] // pool), spare)
            holding[i] = holding[i] + addition
            spare = spare - addition
    return np.array([limit] + holding)


def ragged(rng, amount, total, limit, skew):
    if amount == 2:
        one = jax.random.randint(rng, (), max(1, total - limit), min(limit, total - 1) + 1)
        return jnp.stack([one, total - one])
    tallies = jnp.asarray(split_up(amount, total, limit, skew), jnp.int32)
    twos = (amount - 1) // 2
    giver, receiver = tallies[1:1 + 2 * twos:2], tallies[2:2 + 2 * twos:2]
    margin = jnp.minimum(giver - 1, limit - receiver)
    moved = jax.random.randint(jax.random.fold_in(rng, 1), (twos,), 0, 1 << 20) % (margin + 1)
    tallies = tallies.at[1:1 + 2 * twos:2].set(giver - moved).at[2:2 + 2 * twos:2].set(receiver + moved)
    return tallies[jax.random.permutation(jax.random.fold_in(rng, 2), amount)]


def scatter_about(rng, dims, width, reach, held_as=jnp.bfloat16):
    array = width * jax.random.normal(rng, dims, jnp.float32)
    return jnp.clip(array, min=-reach, max=reach).astype(held_as)


def setup_inputs(seed: int = 0, part: int = 0) -> dict:
    splits = jax.random.split(jax.random.key(seed), 13)
    own_keys = jax.random.split(jax.random.fold_in(splits[12], part), 13)
    pair = draw_pair(jax.random.fold_in(jax.random.fold_in(splits[12], part), 71), part)
    pair_mask = set_ends((jax.random.randint(own_keys[1], (N_RES, N_RES), 0, 8) < 7).astype(jnp.int32), jax.random.fold_in(own_keys[1], 1), 0, 1)
    chain_ids = jnp.searchsorted(jnp.cumsum(ragged(own_keys[2], 4, N_RES, N_RES // 2, 1)), jnp.arange(N_RES), side="right").astype(jnp.int32)
    norm_gain = jnp.clip(1.0 + 0.1 * jax.random.normal(splits[3], (3, C), jnp.float32), 0.5, 1.5)
    norm_shift = scatter_about(splits[4], (3, C), 0.5, 3.0, jnp.float32)
    attn_proj = scatter_about(splits[5], (2, C, 4 * HEADS * HEAD_DIM), (C // 4) ** -0.5, 1.0)
    gate_shift = scatter_about(splits[6], (2, HEADS * HEAD_DIM), 1.0, 4.0, jnp.float32)
    bias_proj = draw_bias_proj(jax.random.fold_in(splits[12], 71), part)
    chain_scale = draw_chain_scale(jax.random.fold_in(splits[12], 71), part)
    attn_out = scatter_about(splits[9], (2, HEADS * HEAD_DIM, C), (HEADS * HEAD_DIM) ** -0.5, 0.5)
    trans_in = scatter_about(splits[10], (C, TRANS), C ** -0.5, 0.5)
    trans_out = scatter_about(splits[11], (TRANS, C), TRANS ** -0.5, 0.25)
    return dict(pair=pair, pair_mask=pair_mask, chain_ids=chain_ids, norm_gain=norm_gain, norm_shift=norm_shift, attn_proj=attn_proj, gate_shift=gate_shift, bias_proj=bias_proj, chain_scale=chain_scale, attn_out=attn_out, trans_in=trans_in, trans_out=trans_out)


def normalize(x, gain, shift):
    mean = lax.optimization_barrier(jnp.mean(x, axis=-1, keepdims=True))
    center = x - mean
    var = lax.optimization_barrier(jnp.mean(center * center, axis=-1, keepdims=True))
    return center * lax.rsqrt(var + 1e-05) * gain + shift

def attend_block(x_row, query, keys, values, gate, bias, extra, mask_row, w_out):
    scores = jnp.einsum('jhd,khd->hjk', query.astype(jnp.float32), keys.astype(jnp.float32))
    logits = scores + bias + extra + mask_row[None, None, :]
    top = lax.optimization_barrier(jnp.max(logits, axis=-1, keepdims=True))
    expd = jnp.exp(logits - top)
    weights = (expd / lax.optimization_barrier(jnp.sum(expd, axis=-1, keepdims=True))).astype(jnp.bfloat16)
    mixed = jnp.einsum('hjk,khd->jhd', weights.astype(jnp.float32), values.astype(jnp.float32))
    gated = (mixed * gate).astype(jnp.bfloat16).reshape(query.shape[0], HEADS * HEAD_DIM)
    return (x_row + jnp.dot(gated, w_out, preferred_element_type=jnp.float32)).astype(jnp.bfloat16)

def triangle(pair, mask, chain_ids, layer, norm_gain, norm_shift, attn_proj, gate_shift, bias_proj, chain_scale, attn_out):
    hidden = HEADS * HEAD_DIM
    x = pair.astype(jnp.float32)
    normed = normalize(x, norm_gain[layer], norm_shift[layer]).astype(jnp.bfloat16)
    flat = normed.reshape(N_RES * N_RES, C)
    proj = jnp.dot(flat, attn_proj[layer], preferred_element_type=jnp.float32).reshape(N_RES, N_RES, 4 * hidden)
    shape = (N_RES, N_RES, HEADS, HEAD_DIM)
    query = (proj[..., :hidden] * HEAD_DIM ** (-0.5)).astype(jnp.bfloat16).reshape(shape)
    keys = proj[..., hidden:2 * hidden].astype(jnp.bfloat16).reshape(shape)
    values = proj[..., 2 * hidden:3 * hidden].astype(jnp.bfloat16).reshape(shape)
    gate = jax.nn.sigmoid(proj[..., 3 * hidden:] + gate_shift[layer]).reshape(shape)
    bias = jnp.dot(flat, bias_proj[layer], preferred_element_type=jnp.float32)
    bias = bias.reshape(N_RES, N_RES, HEADS).transpose(2, 0, 1)
    same = (chain_ids[:, None] == chain_ids[None, :]).astype(jnp.float32)
    extra = chain_scale[layer][:, None, None] * same[None]
    mask_term = (mask.astype(jnp.float32) - 1.0) * 1000000000.0

    def one_row(items):
        x_row, q_row, k_row, v_row, g_row, m_row = items
        return attend_block(x_row, q_row, k_row, v_row, g_row, bias, extra, m_row, attn_out[layer])
    return lax.map(one_row, (x, query, keys, values, gate, mask_term))

def reference(pair, pair_mask, chain_ids, norm_gain, norm_shift, attn_proj, gate_shift, bias_proj, chain_scale, attn_out, trans_in, trans_out):
    params = (norm_gain, norm_shift, attn_proj, gate_shift, bias_proj, chain_scale, attn_out)
    start = triangle(pair, pair_mask, chain_ids, 0, *params)
    ending = triangle(start.transpose(1, 0, 2), pair_mask.T, chain_ids, 1, *params).transpose(1, 0, 2)
    y = ending.astype(jnp.float32)
    flat_y = y.reshape(N_RES * N_RES, C)
    normed = normalize(flat_y, norm_gain[2], norm_shift[2]).astype(jnp.bfloat16)
    inner = jax.nn.relu(jnp.dot(normed, trans_in, preferred_element_type=jnp.float32)).astype(jnp.bfloat16)
    out = flat_y + jnp.dot(inner, trans_out, preferred_element_type=jnp.float32)
    return out.astype(jnp.bfloat16).reshape(N_RES, N_RES, C)
```

```python
import functools

import jax
import jax.numpy as jnp
from jax import lax
from jax.experimental import pallas as pl
from jax.experimental.pallas import tpu as pltpu
from jax.sharding import PartitionSpec as P

C = 128
HEADS = 4
DX = (0, 0, 2, 1, 3, 1, 3, 2)
DY = (0, 1, 0, 0, 0, 1, 1, 1)
F32 = jnp.float32
BF16 = jnp.bfloat16
NT = (((1,), (1,)), ((), ()))


def layer_norm(x, gain, shift):
    mean = jnp.mean(x, axis=-1, keepdims=True)
    center = x - mean
    var = jnp.mean(center * center, axis=-1, keepdims=True)
    return center * lax.rsqrt(var + 1e-05) * gain + shift


def pick(t, table):
    value = jnp.int32(table[0])
    for index in range(1, len(table)):
        value = jnp.where(t == index, jnp.int32(table[index]), value)
    return value


def kernel(
    nz,
    pair,
    mask,
    cid,
    gain,
    shift,
    wp,
    gsh,
    bp,
    wo,
    ti,
    to,
    scale,
    out,
    xs,
    xt,
    xn,
    q,
    k,
    vo,
    gate,
    bt,
    bx,
    gs,
    mrow,
    cidc,
    mz,
    mt,
    mrecv,
    planes,
    stage,
    recv,
    z_send,
    z_recv,
    p_send,
    p_recv,
    a_send,
    a_recv,
    m_send,
    m_recv,
    l_sem,
):
    n = pair.shape[1]
    nd = 8 * nz
    rows = 8 * nz
    group = 128 // rows
    me = lax.axis_index("dap")
    z = lax.rem(me, nz)
    pm = lax.div(me, nz)
    xx = lax.div(pm, 2)
    yy = lax.rem(pm, 2)

    def plane(dx, dy):
        return lax.rem(xx + dx, 4) * 2 + lax.rem(yy + dy, 2)

    def send(src, dst, send_sem, recv_sem, dest):
        pltpu.make_async_remote_copy(
            src_ref=src,
            dst_ref=dst,
            send_sem=send_sem,
            recv_sem=recv_sem,
            device_id={"dap": dest},
            device_id_type=pl.DeviceIdType.MESH,
        ).start()

    def drain(ref, sem):
        pltpu.make_async_copy(ref, ref, sem).wait()

    mz[...] = jnp.zeros_like(mz)
    barrier = pltpu.get_barrier_semaphore()

    def greet(d, carry):
        pl.semaphore_signal(
            barrier,
            inc=1,
            device_id={"dap": lax.rem(me + d, nd)},
            device_id_type=pl.DeviceIdType.MESH,
        )
        return carry

    lax.fori_loop(1, nd, greet, 0)

    lane_head = lax.div(lax.broadcasted_iota(jnp.int32, (1, 1, C), 2), 32)
    cid_row = cid[...].astype(F32)
    cidc[...] = jnp.transpose(jnp.broadcast_to(cid_row, (128, n)))
    mask_f = mask[...].astype(F32)
    mrow[0] = (mask_f - 1.0) * 1e9
    ones = jnp.ones((n, C), BF16)
    for r in range(8):
        vo[r, :, C:] = ones

    for layer in range(2):
        g_l, s_l = gain[layer : layer + 1, :], shift[layer : layer + 1, :]
        if layer == 1:
            def unpack(s, carry):
                xt[pl.ds(pl.multiple_of(s * 64, 64), 64), :] = recv[0, s].astype(F32)
                return carry

            lax.fori_loop(0, nd, unpack, 0, unroll=8)

        def norm_row(r, carry):
            if layer == 0:
                x = pair[r].astype(F32)
            else:
                x = xt[pl.ds(r, n, stride=8), :]
            xs[r] = x
            xnv = layer_norm(x, g_l, s_l).astype(BF16)
            xn[r] = xnv
            b = lax.dot_general(bp[layer], xnv, NT, preferred_element_type=F32)
            for c in range(n // 128):
                bt[c, pl.ds(pl.multiple_of(r * 8, 8), 4), :] = b[:, c * 128 : (c + 1) * 128]
            return carry

        lax.fori_loop(0, 8, norm_row, 0)
        for c in range(n // 128):
            own = [bt[c, pl.ds(h, 8, stride=8), :] for h in range(HEADS)]
            own = jnp.concatenate(own, axis=0).astype(BF16)
            planes[layer, pm, z, :, c * 128 : (c + 1) * 128] = own

        if layer == 0:
            pl.semaphore_wait(barrier, nd - 1)
        for d in range(1, nz):
            ref = planes.at[layer, pm, z]
            send(ref, ref, z_send.at[layer], z_recv.at[layer], pm * nz + lax.rem(z + d, nz))
        if layer == 0:
            at = pl.ds(pl.multiple_of(lax.rem(pm, group) * rows + z * 8, 8), 8)
            mz[at, :] = mask_f
            for d in range(1, nz):
                ref = mz.at[at, :]
                send(ref, ref, m_send.at[0], m_recv.at[0], pm * nz + lax.rem(z + d, nz))

        gate_shift = gsh[layer : layer + 1, :]

        def project(r, carry):
            f = jnp.dot(xn[r], wp[layer], preferred_element_type=F32)
            q[r] = f[:, :C] * (32 ** -0.5)
            k[r] = f[:, C : 2 * C].astype(BF16)
            vo[r, :, :C] = f[:, 2 * C : 3 * C].astype(BF16)
            gate[r] = jax.nn.sigmoid(f[:, 3 * C :] + gate_shift)
            return carry

        lax.fori_loop(0, 8, project, 0)

        drain(planes.at[layer, pm, pl.ds(0, nz - 1)], z_recv.at[layer])
        for dx, dy in ((0, 1), (2, 0), (1, 0), (3, 0)):
            ref = planes.at[layer, pm]
            send(ref, ref, p_send.at[layer], p_recv.at[layer, pm], plane(dx, dy) * nz + z)
        if layer == 0:
            drain(mz.at[pl.ds(0, (nz - 1) * 8)], m_recv.at[0])
            mt[...] = jnp.transpose(mz[...])
            for t in range(1, 8):
                pt = plane(DX[t], DY[t])
                src = mt.at[pl.ds(pl.multiple_of((pt * nz + z) * 8, 8), 8), :]
                send(src, mrecv.at[pm], m_send.at[1], m_recv.at[1], pt * nz + z)
            mrecv[pm] = mt[pl.ds(pl.multiple_of(me * 8, 8), 8), :]

        def block(t, carry):
            m = plane(pick(t, DX), pick(t, DY))

            @pl.when(t > 0)
            def _():
                drain(planes.at[layer, m], p_recv.at[layer, m])

            @pl.when(t == 1)
            def _():
                for dx in (1, 3):
                    ref = planes.at[layer, m]
                    send(ref, ref, p_send.at[layer], p_recv.at[layer, m], plane(dx, 0) * nz + z)

            @pl.when(t == 2)
            def _():
                ref = planes.at[layer, m]
                send(ref, ref, p_send.at[layer], p_recv.at[layer, m], plane(0, 1) * nz + z)

            here = pl.ds(pl.multiple_of(m * rows, rows), rows)
            cb = cidc[here, :]
            for c in range(n // 128):
                lanes = slice(c * 128, (c + 1) * 128)
                same = jnp.where(cb == cid_row[:, lanes], 1.0, 0.0).reshape(nz, 8, 128)
                b = planes[layer, m, :, :, lanes].astype(F32).reshape(nz, HEADS, 8, 128)
                b = jnp.stack(
                    [b[:, h] + scale[layer, h] * same for h in range(HEADS)], axis=1
                )
                bx[:, lanes] = b.reshape(4 * rows, 128)

            for i in range(8):
                qi = q[i, here, :].reshape(nz, 8, C)
                qm = jnp.stack(
                    [jnp.where(lane_head == h, qi, 0.0) for h in range(HEADS)], axis=1
                )
                qm = qm.reshape(4 * rows, C).astype(BF16)
                s = lax.dot_general(qm, k[i], NT, preferred_element_type=F32)
                s = s + bx[...] + mrow[layer, i : i + 1, :]
                top = jnp.max(s, axis=-1, keepdims=True)
                p = jnp.exp(s - top).astype(BF16)
                o = jnp.dot(p, vo[i], preferred_element_type=F32)
                o = o.reshape(nz, HEADS, 8, 2 * C)
                mixed, total = o[:, 0, :, :C], o[:, 0, :, C:]
                for h in range(1, HEADS):
                    mixed = jnp.where(lane_head == h, o[:, h, :, :C], mixed)
                    total = jnp.where(lane_head == h, o[:, h, :, C:], total)
                weighted = (mixed / total).reshape(rows, C) * gate[i, here, :]
                gs[i * rows : (i + 1) * rows, :] = weighted.astype(BF16)

            y = jnp.dot(gs[...], wo[layer], preferred_element_type=F32)
            y = y + xs[:, here, :].reshape(8 * rows, C)
            if layer == 1:
                y = y.astype(BF16).astype(F32)
                yn = layer_norm(y, gain[2:3, :], shift[2:3, :]).astype(BF16)
                inner = jnp.dot(yn, ti[...], preferred_element_type=F32)
                inner = jnp.maximum(inner, 0.0).astype(BF16)
                y = y + jnp.dot(inner, to[...], preferred_element_type=F32)
            y = y.reshape(8, nz, 8, C)
            for zz in range(nz):
                stage[layer, m, zz] = y[:, zz].reshape(64, C).astype(BF16)

            for d in range(nz):
                zt = lax.rem(z + d, nz)

                def go(zt=zt):
                    send(
                        stage.at[layer, m, zt],
                        recv.at[layer, me],
                        a_send.at[layer],
                        a_recv.at[layer],
                        m * nz + zt,
                    )

                if d == 0:
                    pl.when(t > 0)(go)

                    @pl.when(t == 0)
                    def _():
                        copy = pltpu.make_async_copy(
                            stage.at[layer, m, z], recv.at[layer, me], l_sem
                        )
                        copy.start()
                        copy.wait()
                else:
                    go()
            return carry

        lax.fori_loop(0, 8, block, 0)

        if layer == 0:
            drain(mrecv.at[pl.ds(0, 7)], m_recv.at[1])
            parts = []
            for c in range(n // 128):
                part = mrecv[c * group]
                for g in range(1, group):
                    part = part + mrecv[c * group + g]
                parts.append(part)
            mrow[1] = (jnp.concatenate(parts, axis=1) - 1.0) * 1e9
        drain(recv.at[layer, pl.ds(0, nd - 1)], a_recv.at[layer])

    def unpack_last(s, carry):
        xt[pl.ds(pl.multiple_of(s * 64, 64), 64), :] = recv[1, s].astype(F32)
        return carry

    lax.fori_loop(0, nd, unpack_last, 0, unroll=8)
    for r in range(8):
        out[r] = xt[pl.ds(r, n, stride=8), :].astype(BF16)

    for layer in range(2):
        drain(planes.at[layer, 0, pl.ds(0, nz - 1)], z_send.at[layer])
        drain(planes.at[layer, pl.ds(0, 7)], p_send.at[layer])
        drain(recv.at[layer, pl.ds(0, nd - 1)], a_send.at[layer])
    drain(mz.at[pl.ds(0, (nz - 1) * 8)], m_send.at[0])
    drain(mrecv.at[pl.ds(0, 7)], m_send.at[1])


def body(
    pair,
    pair_mask,
    chain_ids,
    norm_gain,
    norm_shift,
    attn_proj,
    gate_shift,
    bias_proj,
    chain_scale,
    attn_out,
    trans_in,
    trans_out,
):
    n = pair.shape[1]
    nz = n // 64
    rows = 8 * nz
    vmem = pl.BlockSpec(memory_space=pltpu.VMEM)
    smem = pl.BlockSpec(memory_space=pltpu.SMEM)
    dma = pltpu.SemaphoreType.DMA
    return pl.pallas_call(
        functools.partial(kernel, nz),
        out_shape=jax.ShapeDtypeStruct(pair.shape, BF16),
        in_specs=[vmem] * 11 + [smem],
        out_specs=vmem,
        scratch_shapes=[
            pltpu.VMEM((8, n, C), F32),
            pltpu.VMEM((8 * n, C), F32),
            pltpu.VMEM((8, n, C), BF16),
            pltpu.VMEM((8, n, C), F32),
            pltpu.VMEM((8, n, C), BF16),
            pltpu.VMEM((8, n, 2 * C), BF16),
            pltpu.VMEM((8, n, C), F32),
            pltpu.VMEM((n // 128, 64, 128), F32),
            pltpu.VMEM((4 * rows, n), F32),
            pltpu.VMEM((8 * rows, C), BF16),
            pltpu.VMEM((2, 8, n), F32),
            pltpu.VMEM((n, 128), F32),
            pltpu.VMEM((128, n), F32),
            pltpu.VMEM((n, 128), F32),
            pltpu.VMEM((8, 8, 128), F32),
            pltpu.VMEM((2, 8, nz, 32, n), BF16),
            pltpu.VMEM((2, 8, nz, 64, C), BF16),
            pltpu.VMEM((2, 8 * nz, 64, C), BF16),
            dma((2,)),
            dma((2,)),
            dma((2,)),
            dma((2, 8)),
            dma((2,)),
            dma((2,)),
            dma((2,)),
            dma((2,)),
            dma,
        ],
        compiler_params=pltpu.CompilerParams(
            collective_id=0,
            has_side_effects=True,
            vmem_limit_bytes=56 * 1024 * 1024,
        ),
    )(
        pair,
        pair_mask,
        chain_ids.reshape(1, n),
        norm_gain,
        norm_shift,
        attn_proj,
        gate_shift,
        jnp.swapaxes(bias_proj, 1, 2),
        attn_out,
        trans_in,
        trans_out,
        chain_scale,
    )


def solution(mesh):
    in_specs = (
        P(("rep", "dap"), None, None),
        P(("rep", "dap"), None),
        P("rep"),
    ) + (P(),) * 9
    out_specs = P(("rep", "dap"), None, None)
    return jax.shard_map(body, mesh=mesh, in_specs=in_specs, out_specs=out_specs, check_vma=False)
```

```python
import functools

import jax
import jax.numpy as jnp
from jax import lax
from jax.experimental import pallas as pl
from jax.experimental.pallas import tpu as pltpu
from jax.sharding import PartitionSpec as P

C = 128
HEADS = 4
NZ = 8
ND = 64
N = 512
ROWS = 64
DX = (0, 0, 1, 3, 1, 3, 2, 2)
DY = (0, 1, 0, 0, 1, 1, 0, 1)
F32 = jnp.float32
BF16 = jnp.bfloat16
NT = (((1,), (1,)), ((), ()))


def layer_norm(x, gain, shift):
    mean = jnp.mean(x, axis=-1, keepdims=True)
    center = x - mean
    var = jnp.mean(center * center, axis=-1, keepdims=True)
    return center * lax.rsqrt(var + 1e-05) * gain + shift


def pick(t, table):
    value = jnp.int32(table[0])
    for index in range(1, len(table)):
        value = jnp.where(t == index, jnp.int32(table[index]), value)
    return value


def kernel(
    pair,
    mask,
    cid,
    gain,
    shift,
    wp,
    gsh,
    bp,
    wo,
    ti,
    to,
    scale,
    out,
    xs,
    xt,
    xn,
    q,
    k,
    vo,
    gate,
    bt,
    bx,
    gs,
    mrow,
    cidc,
    mz,
    mt,
    mrecv,
    planes,
    stage,
    recv,
    z_send,
    z_recv,
    p_send,
    p_recv,
    a_send,
    a_recv,
    m_send,
    m_recv,
    l_sem,
):
    me = lax.axis_index("dap")
    z = lax.rem(me, NZ)
    pm = lax.div(me, NZ)
    xx = lax.div(pm, 2)
    yy = lax.rem(pm, 2)

    def plane(dx, dy):
        return lax.rem(xx + dx, 4) * 2 + lax.rem(yy + dy, 2)

    def send(src, dst, send_sem, recv_sem, dest):
        pltpu.make_async_remote_copy(
            src_ref=src,
            dst_ref=dst,
            send_sem=send_sem,
            recv_sem=recv_sem,
            device_id={"dap": dest},
            device_id_type=pl.DeviceIdType.MESH,
        ).start()

    def drain(ref, sem):
        pltpu.make_async_copy(ref, ref, sem).wait()

    mz[...] = jnp.zeros_like(mz)
    barrier = pltpu.get_barrier_semaphore()

    def greet(d, carry):
        pl.semaphore_signal(
            barrier,
            inc=1,
            device_id={"dap": lax.rem(me + d, ND)},
            device_id_type=pl.DeviceIdType.MESH,
        )
        return carry

    lax.fori_loop(1, ND, greet, 0)
    mask_f = mask[...].astype(F32)
    mz_at = pl.ds(pl.multiple_of(yy * ROWS + z * 8, 8), 8)
    mz[mz_at, :] = mask_f
    lane_head = lax.div(lax.broadcasted_iota(jnp.int32, (1, 1, C), 2), 32)
    cid_row = cid[...].astype(F32)

    def lanes_of(index):
        return pl.ds(pl.multiple_of(index * 128, 128), 128)

    def norm(layer, at, x):
        xs[layer, :, lanes_of(at), :] = x.reshape(8, 128, C)
        xnv = layer_norm(x, gain[layer : layer + 1, :], shift[layer : layer + 1, :]).astype(BF16)
        xn[at] = xnv
        b = lax.dot_general(bp[layer], xnv, NT, preferred_element_type=F32)
        for r in range(8):
            bt[r * 8 : r * 8 + 4, :] = b[:, r * 128 : (r + 1) * 128]
        own = [bt[pl.ds(h, 8, stride=8), :] for h in range(HEADS)]
        planes[layer, pm, z, at] = jnp.concatenate(own, axis=0).astype(BF16)
        if layer == 0:
            return
        for d in range(1, NZ):
            ref = planes.at[layer, pm, z, at]
            send(ref, ref, z_send.at[layer], z_recv.at[layer, d], pm * NZ + lax.rem(z + d, NZ))

    def project(layer, at):
        f = jnp.dot(xn[at], wp[layer], preferred_element_type=F32)
        here = lanes_of(at)
        q[layer, :, here, :] = (f[:, :C] * (32 ** -0.5)).reshape(8, 128, C)
        k[layer, :, here, :] = f[:, C : 2 * C].astype(BF16).reshape(8, 128, C)
        vo[layer, :, here, :C] = f[:, 2 * C : 3 * C].astype(BF16).reshape(8, 128, C)
        g = jax.nn.sigmoid(f[:, 3 * C :] + gsh[layer : layer + 1, :])
        gate[layer, :, here, :] = g.reshape(8, 128, C)

    def arrive(layer, dx):
        source = lax.rem(xx + 4 - dx, 4)
        for yh in range(2):
            m = source * 2 + yh

            @pl.when(m == pm)
            def _():
                drain(recv.at[layer, pl.ds(0, NZ - 1)], a_recv.at[layer, m])

            @pl.when(m != pm)
            def _():
                drain(recv.at[layer, pl.ds(0, NZ)], a_recv.at[layer, m])

        for s in range(16):
            xt[s * 64 : (s + 1) * 64, :] = recv[layer, source * 16 + s].astype(F32)
        columns = [xt[pl.ds(c, 128, stride=8), :] for c in range(8)]
        if layer == 0:
            norm(1, source, jnp.concatenate(columns, axis=0))
        else:
            for i in range(8):
                out[i, lanes_of(source), :] = columns[i].astype(BF16)

    def first_norm(at, carry):
        norm(0, at, pair[:, lanes_of(at), :].astype(F32).reshape(1024, C))
        return carry

    lax.fori_loop(0, 4, first_norm, 0)
    pl.semaphore_wait(barrier, ND - 1)
    def share(ref, layer, m, offsets):
        for dx, dy in offsets:
            send(ref, ref, p_send.at[layer], p_recv.at[layer, m], plane(dx, dy) * NZ + z)

    def share_piece(layer, d):
        source = lax.rem(z + NZ - d, NZ)
        ref = planes.at[layer, pm, source]
        if d:
            drain(ref, z_recv.at[layer, d])
        share(ref, layer, pm, ((0, 1), (1, 0), (3, 0), (2, 0)))

    for d in (1, 7, 2, 6, 3, 5, 4):
        ref = planes.at[0, pm, z]
        send(ref, ref, z_send.at[0], z_recv.at[0, d], pm * NZ + lax.rem(z + d, NZ))
    share_piece(0, 0)
    project(0, 0)
    share_piece(0, 1)
    share_piece(0, 7)
    project(0, 1)
    share_piece(0, 2)
    share_piece(0, 6)
    project(0, 2)
    share_piece(0, 3)
    share_piece(0, 5)
    project(0, 3)
    cidc[...] = jnp.transpose(jnp.broadcast_to(cid_row, (128, N)))
    mrow[0] = (mask_f - 1.0) * 1e9
    ones = jnp.ones((N, C), BF16)
    for layer in range(2):
        for r in range(8):
            vo[layer, r, :, C:] = ones

    share_piece(0, 4)
    for d in range(1, NZ):
        ref = mz.at[mz_at, :]
        send(ref, ref, m_send.at[0], m_recv.at[0], pm * NZ + lax.rem(z + d, NZ))

    for layer in range(2):
        if layer == 1:
            for d in (0, 1, 7, 2, 6, 3, 5, 4):
                share_piece(1, d)

        def block(t, carry):
            m = plane(pick(t, DX), pick(t, DY))

            @pl.when((t > 0) & (t != 6))
            def _():
                drain(planes.at[layer, m], p_recv.at[layer, m])

            @pl.when(t == 1)
            def _():
                share(planes.at[layer, m], layer, m, ((1, 0), (3, 0)))

            @pl.when(t == 3)
            def _():
                far = plane(2, 0)
                ref = planes.at[layer, far]
                drain(ref, p_recv.at[layer, far])
                share(ref, layer, far, ((0, 1),))

            here = pl.ds(pl.multiple_of(m * ROWS, ROWS), ROWS)
            cb = cidc[here, :]
            for c in range(N // 128):
                lanes = slice(c * 128, (c + 1) * 128)
                same = jnp.where(cb == cid_row[:, lanes], 1.0, 0.0).reshape(NZ, 8, 128)
                b = planes[layer, m, :, c].astype(F32).reshape(NZ, HEADS, 8, 128)
                b = jnp.stack(
                    [b[:, h] + scale[layer, h] * same for h in range(HEADS)], axis=1
                )
                bx[:, lanes] = b.reshape(4 * ROWS, 128)

            for i in range(8):
                qi = q[layer, i, here, :].reshape(NZ, 8, C)
                qm = jnp.stack(
                    [jnp.where(lane_head == h, qi, 0.0) for h in range(HEADS)], axis=1
                )
                qm = qm.reshape(4 * ROWS, C).astype(BF16)
                s = lax.dot_general(qm, k[layer, i], NT, preferred_element_type=F32)
                s = s + bx[...] + mrow[layer, i : i + 1, :]
                top = jnp.max(s, axis=-1, keepdims=True)
                p = jnp.exp(s - top).astype(BF16)
                o = jnp.dot(p, vo[layer, i], preferred_element_type=F32)
                o = o.reshape(NZ, HEADS, 8, 2 * C)
                mixed, total = o[:, 0, :, :C], o[:, 0, :, C:]
                for h in range(1, HEADS):
                    mixed = jnp.where(lane_head == h, o[:, h, :, :C], mixed)
                    total = jnp.where(lane_head == h, o[:, h, :, C:], total)
                weighted = (mixed / total).reshape(ROWS, C) * gate[layer, i, here, :]
                gs[i * ROWS : (i + 1) * ROWS, :] = weighted.astype(BF16)

            y = jnp.dot(gs[...], wo[layer], preferred_element_type=F32)
            y = y + xs[layer, :, here, :].reshape(8 * ROWS, C)
            if layer == 1:
                y = y.astype(BF16).astype(F32)
                yn = layer_norm(y, gain[2:3, :], shift[2:3, :]).astype(BF16)
                inner = jnp.dot(yn, ti[...], preferred_element_type=F32)
                inner = jnp.maximum(inner, 0.0).astype(BF16)
                y = y + jnp.dot(inner, to[...], preferred_element_type=F32)
            y = y.reshape(8, NZ, 8, C)
            for zz in range(NZ):
                stage[layer, m, zz] = y[:, zz].reshape(64, C).astype(BF16)

            for d in range(NZ):
                zt = lax.rem(z + d, NZ)

                def go(zt=zt):
                    send(
                        stage.at[layer, m, zt],
                        recv.at[layer, me],
                        a_send.at[layer],
                        a_recv.at[layer, pm],
                        m * NZ + zt,
                    )

                if d == 0:
                    pl.when(t > 0)(go)

                    @pl.when(t == 0)
                    def _():
                        copy = pltpu.make_async_copy(
                            stage.at[layer, m, z], recv.at[layer, me], l_sem
                        )
                        copy.start()
                        copy.wait()
                else:
                    go()

            if layer == 0:

                @pl.when(t == 2)
                def _():
                    drain(mz.at[pl.ds(0, (NZ - 1) * 8)], m_recv.at[0])
                    mt[...] = jnp.transpose(mz[...])
                    for j in range(1, 8):
                        pt = plane(DX[j], DY[j])
                        src = mt.at[pl.ds(pl.multiple_of((pt * NZ + z) * 8, 8), 8), :]
                        send(src, mrecv.at[pm], m_send.at[1], m_recv.at[1], pt * NZ + z)
                    mrecv[pm] = mt[pl.ds(pl.multiple_of(me * 8, 8), 8), :]

            return carry

        lax.fori_loop(0, 8, block, 0)

        def late(index, carry):
            arrive(layer, pick(index, (0, 1, 3, 2)))
            if layer == 0:

                @pl.when(index > 0)
                def _():
                    project(1, lax.rem(xx + 4 - pick(index, (0, 0, 1, 3)), 4))

            return carry

        lax.fori_loop(0, 4, late, 0)
        if layer == 0:
            project(1, lax.rem(xx + 2, 4))
        if layer == 0:
            drain(mrecv.at[pl.ds(0, 7)], m_recv.at[1])
            parts = [mrecv[2 * c] + mrecv[2 * c + 1] for c in range(N // 128)]
            mrow[1] = (jnp.concatenate(parts, axis=1) - 1.0) * 1e9

    for layer in range(2):
        drain(planes.at[layer, 0, pl.ds(0, NZ - 1)], z_send.at[layer])
        drain(planes.at[layer, pl.ds(0, 7)], p_send.at[layer])
        drain(recv.at[layer, pl.ds(0, ND - 1)], a_send.at[layer])
    drain(mz.at[pl.ds(0, (NZ - 1) * 8)], m_send.at[0])
    drain(mrecv.at[pl.ds(0, 7)], m_send.at[1])


def body(
    pair,
    pair_mask,
    chain_ids,
    norm_gain,
    norm_shift,
    attn_proj,
    gate_shift,
    bias_proj,
    chain_scale,
    attn_out,
    trans_in,
    trans_out,
):
    vmem = pl.BlockSpec(memory_space=pltpu.VMEM)
    smem = pl.BlockSpec(memory_space=pltpu.SMEM)
    dma = pltpu.SemaphoreType.DMA
    return pl.pallas_call(
        kernel,
        out_shape=jax.ShapeDtypeStruct(pair.shape, BF16),
        in_specs=[vmem] * 11 + [smem],
        out_specs=vmem,
        scratch_shapes=[
            pltpu.VMEM((2, 8, N, C), F32),
            pltpu.VMEM((1024, C), F32),
            pltpu.VMEM((4, 1024, C), BF16),
            pltpu.VMEM((2, 8, N, C), F32),
            pltpu.VMEM((2, 8, N, C), BF16),
            pltpu.VMEM((2, 8, N, 2 * C), BF16),
            pltpu.VMEM((2, 8, N, C), F32),
            pltpu.VMEM((64, 128), F32),
            pltpu.VMEM((4 * ROWS, N), F32),
            pltpu.VMEM((8 * ROWS, C), BF16),
            pltpu.VMEM((2, 8, N), F32),
            pltpu.VMEM((N, 128), F32),
            pltpu.VMEM((128, N), F32),
            pltpu.VMEM((N, 128), F32),
            pltpu.VMEM((8, 8, 128), F32),
            pltpu.VMEM((2, 8, NZ, 4, 32, 128), BF16),
            pltpu.VMEM((2, 8, NZ, 64, C), BF16),
            pltpu.VMEM((2, ND, 64, C), BF16),
            dma((2,)),
            dma((2, NZ)),
            dma((2,)),
            dma((2, 8)),
            dma((2,)),
            dma((2, 8)),
            dma((2,)),
            dma((2,)),
            dma,
        ],
        compiler_params=pltpu.CompilerParams(
            collective_id=0,
            has_side_effects=True,
            vmem_limit_bytes=56 * 1024 * 1024,
        ),
    )(
        pair,
        pair_mask,
        chain_ids.reshape(1, N),
        norm_gain,
        norm_shift,
        attn_proj,
        gate_shift,
        jnp.swapaxes(bias_proj, 1, 2),
        attn_out,
        trans_in,
        trans_out,
        chain_scale,
    )


def solution(mesh):
    in_specs = (
        P(("rep", "dap"), None, None),
        P(("rep", "dap"), None),
        P("rep"),
    ) + (P(),) * 9
    out_specs = P(("rep", "dap"), None, None)
    return jax.shard_map(body, mesh=mesh, in_specs=in_specs, out_specs=out_specs, check_vma=False)
```

```python
import functools

import jax
import jax.numpy as jnp
from jax import lax
from jax.experimental import pallas as pl
from jax.experimental.pallas import tpu as pltpu
from jax.sharding import PartitionSpec as P

C = 128
HEADS = 4
NZ = 8
ND = 64
N = 512
ROWS = 64
DX = (0, 0, 1, 3, 1, 3, 2, 2)
DY = (0, 1, 0, 0, 1, 1, 0, 1)
F32 = jnp.float32
BF16 = jnp.bfloat16
NT = (((1,), (1,)), ((), ()))


def layer_norm(x, gain, shift):
    mean = jnp.mean(x, axis=-1, keepdims=True)
    center = x - mean
    var = jnp.mean(center * center, axis=-1, keepdims=True)
    return center * lax.rsqrt(var + 1e-05) * gain + shift


def pick(t, table):
    value = jnp.int32(table[0])
    for index in range(1, len(table)):
        value = jnp.where(t == index, jnp.int32(table[index]), value)
    return value


def kernel(
    pair,
    mask,
    cid,
    gain,
    shift,
    wp,
    gsh,
    bp,
    wo,
    ti,
    to,
    scale,
    out,
    xs,
    xt,
    xn,
    q,
    k,
    vo,
    gate,
    bt,
    bx,
    gs,
    mrow,
    cidc,
    mz,
    mt,
    mrecv,
    planes,
    stage,
    recv,
    z_send,
    z_recv,
    p_send,
    p_recv,
    f_recv,
    a_send,
    a_recv,
    m_send,
    m_recv,
    l_sem,
):
    me = lax.axis_index("dap")
    z = lax.rem(me, NZ)
    pm = lax.div(me, NZ)
    xx = lax.div(pm, 2)
    yy = lax.rem(pm, 2)

    def plane(dx, dy):
        return lax.rem(xx + dx, 4) * 2 + lax.rem(yy + dy, 2)

    def send(src, dst, send_sem, recv_sem, dest):
        pltpu.make_async_remote_copy(
            src_ref=src,
            dst_ref=dst,
            send_sem=send_sem,
            recv_sem=recv_sem,
            device_id={"dap": dest},
            device_id_type=pl.DeviceIdType.MESH,
        ).start()

    def drain(ref, sem):
        pltpu.make_async_copy(ref, ref, sem).wait()

    mz[...] = jnp.zeros_like(mz)
    barrier = pltpu.get_barrier_semaphore()

    def greet(d, carry):
        pl.semaphore_signal(
            barrier,
            inc=1,
            device_id={"dap": lax.rem(me + d, ND)},
            device_id_type=pl.DeviceIdType.MESH,
        )
        return carry

    lax.fori_loop(1, ND, greet, 0)
    mask_f = mask[...].astype(F32)
    mz_at = pl.ds(pl.multiple_of(yy * ROWS + z * 8, 8), 8)
    mz[mz_at, :] = mask_f
    lane_head = lax.div(lax.broadcasted_iota(jnp.int32, (1, 1, C), 2), 32)
    cid_row = cid[...].astype(F32)

    def lanes_of(index):
        return pl.ds(pl.multiple_of(index * 128, 128), 128)

    def norm(layer, at, x):
        xs[layer, :, lanes_of(at), :] = x.reshape(8, 128, C)
        xnv = layer_norm(x, gain[layer : layer + 1, :], shift[layer : layer + 1, :]).astype(BF16)
        xn[at] = xnv
        b = lax.dot_general(bp[layer], xnv, NT, preferred_element_type=F32)
        for r in range(8):
            bt[r * 8 : r * 8 + 4, :] = b[:, r * 128 : (r + 1) * 128]
        own = [bt[pl.ds(h, 8, stride=8), :] for h in range(HEADS)]
        planes[layer, pm, z, at] = jnp.concatenate(own, axis=0).astype(BF16)
        if layer == 0:
            return
        for d in range(1, NZ):
            ref = planes.at[layer, pm, z, at]
            send(ref, ref, z_send.at[layer], z_recv.at[layer, d], pm * NZ + lax.rem(z + d, NZ))
        send(ref, ref, p_send.at[layer], f_recv, plane(2, 0) * NZ + z)

    def project(layer, at):
        f = jnp.dot(xn[at], wp[layer], preferred_element_type=F32)
        here = lanes_of(at)
        q[layer, :, here, :] = (f[:, :C] * (32 ** -0.5)).reshape(8, 128, C)
        k[layer, :, here, :] = f[:, C : 2 * C].astype(BF16).reshape(8, 128, C)
        vo[layer, :, here, :C] = f[:, 2 * C : 3 * C].astype(BF16).reshape(8, 128, C)
        g = jax.nn.sigmoid(f[:, 3 * C :] + gsh[layer : layer + 1, :])
        gate[layer, :, here, :] = g.reshape(8, 128, C)

    def arrive(layer, dx):
        source = lax.rem(xx + 4 - dx, 4)
        for yh in range(2):
            m = source * 2 + yh

            @pl.when(m == pm)
            def _():
                drain(recv.at[layer, pl.ds(0, NZ - 1)], a_recv.at[layer, m])

            @pl.when(m != pm)
            def _():
                drain(recv.at[layer, pl.ds(0, NZ)], a_recv.at[layer, m])

        for s in range(16):
            xt[s * 64 : (s + 1) * 64, :] = recv[layer, source * 16 + s].astype(F32)
        columns = [xt[pl.ds(c, 128, stride=8), :] for c in range(8)]
        if layer == 0:
            norm(1, source, jnp.concatenate(columns, axis=0))
        else:
            for i in range(8):
                out[i, lanes_of(source), :] = columns[i].astype(BF16)

    def first_norm(at, carry):
        norm(0, at, pair[:, lanes_of(at), :].astype(F32).reshape(1024, C))
        return carry

    lax.fori_loop(0, 4, first_norm, 0)
    pl.semaphore_wait(barrier, ND - 1)
    def share(ref, layer, m, offsets):
        for dx, dy in offsets:
            send(ref, ref, p_send.at[layer], p_recv.at[layer, m], plane(dx, dy) * NZ + z)

    def share_piece(layer, d):
        source = lax.rem(z + NZ - d, NZ)
        ref = planes.at[layer, pm, source]
        if d:
            drain(ref, z_recv.at[layer, d])
        near = ((0, 1), (1, 0), (3, 0))
        share(ref, layer, pm, near + ((2, 0),) if layer == 0 else near)

    def spread_far(layer):
        far = plane(2, 0)
        ref = planes.at[layer, far, z]
        drain(ref, f_recv)
        for d in (1, 7, 2, 6, 3, 5, 4):
            send(ref, ref, p_send.at[layer], p_recv.at[layer, far], pm * NZ + lax.rem(z + d, NZ))

    for d in (1, 7, 2, 6, 3, 5, 4):
        ref = planes.at[0, pm, z]
        send(ref, ref, z_send.at[0], z_recv.at[0, d], pm * NZ + lax.rem(z + d, NZ))
    share_piece(0, 0)
    project(0, 0)
    share_piece(0, 1)
    share_piece(0, 7)
    project(0, 1)
    share_piece(0, 2)
    share_piece(0, 6)
    project(0, 2)
    share_piece(0, 3)
    share_piece(0, 5)
    project(0, 3)
    cidc[...] = jnp.transpose(jnp.broadcast_to(cid_row, (128, N)))
    mrow[0] = (mask_f - 1.0) * 1e9
    ones = jnp.ones((N, C), BF16)
    for layer in range(2):
        for r in range(8):
            vo[layer, r, :, C:] = ones

    share_piece(0, 4)
    for d in range(1, NZ):
        ref = mz.at[mz_at, :]
        send(ref, ref, m_send.at[0], m_recv.at[0], pm * NZ + lax.rem(z + d, NZ))

    for layer in range(2):
        if layer == 1:
            spread_far(1)
            for d in (0, 1, 7, 2, 6, 3, 5, 4):
                share_piece(1, d)

        def block(t, carry):
            m = plane(pick(t, DX), pick(t, DY))

            @pl.when((t > 0) & (t != 6))
            def _():
                drain(planes.at[layer, m], p_recv.at[layer, m])

            @pl.when(t == 1)
            def _():
                share(planes.at[layer, m], layer, m, ((1, 0), (3, 0)))

            @pl.when(t == 3)
            def _():
                far = plane(2, 0)
                pieces = NZ if layer == 0 else NZ - 1
                drain(planes.at[layer, far, pl.ds(0, pieces)], p_recv.at[layer, far])
                share(planes.at[layer, far], layer, far, ((0, 1),))

            here = pl.ds(pl.multiple_of(m * ROWS, ROWS), ROWS)
            cb = cidc[here, :]
            for c in range(N // 128):
                lanes = slice(c * 128, (c + 1) * 128)
                same = jnp.where(cb == cid_row[:, lanes], 1.0, 0.0).reshape(NZ, 8, 128)
                b = planes[layer, m, :, c].astype(F32).reshape(NZ, HEADS, 8, 128)
                b = jnp.stack(
                    [b[:, h] + scale[layer, h] * same for h in range(HEADS)], axis=1
                )
                bx[:, lanes] = b.reshape(4 * ROWS, 128)

            for i in range(8):
                qi = q[layer, i, here, :].reshape(NZ, 8, C)
                qm = jnp.stack(
                    [jnp.where(lane_head == h, qi, 0.0) for h in range(HEADS)], axis=1
                )
                qm = qm.reshape(4 * ROWS, C).astype(BF16)
                s = lax.dot_general(qm, k[layer, i], NT, preferred_element_type=F32)
                s = s + bx[...] + mrow[layer, i : i + 1, :]
                top = jnp.max(s, axis=-1, keepdims=True)
                p = jnp.exp(s - top).astype(BF16)
                o = jnp.dot(p, vo[layer, i], preferred_element_type=F32)
                o = o.reshape(NZ, HEADS, 8, 2 * C)
                mixed, total = o[:, 0, :, :C], o[:, 0, :, C:]
                for h in range(1, HEADS):
                    mixed = jnp.where(lane_head == h, o[:, h, :, :C], mixed)
                    total = jnp.where(lane_head == h, o[:, h, :, C:], total)
                weighted = (mixed / total).reshape(ROWS, C) * gate[layer, i, here, :]
                gs[i * ROWS : (i + 1) * ROWS, :] = weighted.astype(BF16)

            y = jnp.dot(gs[...], wo[layer], preferred_element_type=F32)
            y = y + xs[layer, :, here, :].reshape(8 * ROWS, C)
            if layer == 1:
                y = y.astype(BF16).astype(F32)
                yn = layer_norm(y, gain[2:3, :], shift[2:3, :]).astype(BF16)
                inner = jnp.dot(yn, ti[...], preferred_element_type=F32)
                inner = jnp.maximum(inner, 0.0).astype(BF16)
                y = y + jnp.dot(inner, to[...], preferred_element_type=F32)
            y = y.reshape(8, NZ, 8, C)
            for zz in range(NZ):
                stage[layer, m, zz] = y[:, zz].reshape(64, C).astype(BF16)

            for d in range(NZ):
                zt = lax.rem(z + d, NZ)

                def go(zt=zt):
                    send(
                        stage.at[layer, m, zt],
                        recv.at[layer, me],
                        a_send.at[layer],
                        a_recv.at[layer, pm],
                        m * NZ + zt,
                    )

                if d == 0:
                    pl.when(t > 0)(go)

                    @pl.when(t == 0)
                    def _():
                        copy = pltpu.make_async_copy(
                            stage.at[layer, m, z], recv.at[layer, me], l_sem
                        )
                        copy.start()
                        copy.wait()
                else:
                    go()

            if layer == 0:

                @pl.when(t == 2)
                def _():
                    drain(mz.at[pl.ds(0, (NZ - 1) * 8)], m_recv.at[0])
                    mt[...] = jnp.transpose(mz[...])
                    for j in range(1, 8):
                        pt = plane(DX[j], DY[j])
                        src = mt.at[pl.ds(pl.multiple_of((pt * NZ + z) * 8, 8), 8), :]
                        send(src, mrecv.at[pm], m_send.at[1], m_recv.at[1], pt * NZ + z)
                    mrecv[pm] = mt[pl.ds(pl.multiple_of(me * 8, 8), 8), :]

            return carry

        lax.fori_loop(0, 8, block, 0)

        def late(index, carry):
            arrive(layer, pick(index, (0, 1, 3, 2)))
            if layer == 0:

                @pl.when(index > 0)
                def _():
                    project(1, lax.rem(xx + 4 - pick(index, (0, 0, 1, 3)), 4))

            return carry

        lax.fori_loop(0, 4, late, 0)
        if layer == 0:
            project(1, lax.rem(xx + 2, 4))
        if layer == 0:
            drain(mrecv.at[pl.ds(0, 7)], m_recv.at[1])
            parts = [mrecv[2 * c] + mrecv[2 * c + 1] for c in range(N // 128)]
            mrow[1] = (jnp.concatenate(parts, axis=1) - 1.0) * 1e9

    for layer in range(2):
        drain(planes.at[layer, 0, pl.ds(0, NZ - 1)], z_send.at[layer])
        drain(planes.at[layer, pl.ds(0, 7)], p_send.at[layer])
        drain(recv.at[layer, pl.ds(0, ND - 1)], a_send.at[layer])
    drain(mz.at[pl.ds(0, (NZ - 1) * 8)], m_send.at[0])
    drain(mrecv.at[pl.ds(0, 7)], m_send.at[1])


def body(
    pair,
    pair_mask,
    chain_ids,
    norm_gain,
    norm_shift,
    attn_proj,
    gate_shift,
    bias_proj,
    chain_scale,
    attn_out,
    trans_in,
    trans_out,
):
    vmem = pl.BlockSpec(memory_space=pltpu.VMEM)
    smem = pl.BlockSpec(memory_space=pltpu.SMEM)
    dma = pltpu.SemaphoreType.DMA
    return pl.pallas_call(
        kernel,
        out_shape=jax.ShapeDtypeStruct(pair.shape, BF16),
        in_specs=[vmem] * 11 + [smem],
        out_specs=vmem,
        scratch_shapes=[
            pltpu.VMEM((2, 8, N, C), F32),
            pltpu.VMEM((1024, C), F32),
            pltpu.VMEM((4, 1024, C), BF16),
            pltpu.VMEM((2, 8, N, C), F32),
            pltpu.VMEM((2, 8, N, C), BF16),
            pltpu.VMEM((2, 8, N, 2 * C), BF16),
            pltpu.VMEM((2, 8, N, C), F32),
            pltpu.VMEM((64, 128), F32),
            pltpu.VMEM((4 * ROWS, N), F32),
            pltpu.VMEM((8 * ROWS, C), BF16),
            pltpu.VMEM((2, 8, N), F32),
            pltpu.VMEM((N, 128), F32),
            pltpu.VMEM((128, N), F32),
            pltpu.VMEM((N, 128), F32),
            pltpu.VMEM((8, 8, 128), F32),
            pltpu.VMEM((2, 8, NZ, 4, 32, 128), BF16),
            pltpu.VMEM((2, 8, NZ, 64, C), BF16),
            pltpu.VMEM((2, ND, 64, C), BF16),
            dma((2,)),
            dma((2, NZ)),
            dma((2,)),
            dma((2, 8)),
            dma,
            dma((2,)),
            dma((2, 8)),
            dma((2,)),
            dma((2,)),
            dma,
        ],
        compiler_params=pltpu.CompilerParams(
            collective_id=0,
            has_side_effects=True,
            vmem_limit_bytes=56 * 1024 * 1024,
        ),
    )(
        pair,
        pair_mask,
        chain_ids.reshape(1, N),
        norm_gain,
        norm_shift,
        attn_proj,
        gate_shift,
        jnp.swapaxes(bias_proj, 1, 2),
        attn_out,
        trans_in,
        trans_out,
        chain_scale,
    )


def solution(mesh):
    in_specs = (
        P(("rep", "dap"), None, None),
        P(("rep", "dap"), None),
        P("rep"),
    ) + (P(),) * 9
    out_specs = P(("rep", "dap"), None, None)
    return jax.shard_map(body, mesh=mesh, in_specs=in_specs, out_specs=out_specs, check_vma=False)
```

```python
import functools

import jax
import jax.numpy as jnp
from jax import lax
from jax.experimental import pallas as pl
from jax.experimental.pallas import tpu as pltpu
from jax.sharding import PartitionSpec as P

C = 128
HEADS = 4
NZ = 8
ND = 64
N = 512
ROWS = 64
DX = (0, 0, 1, 3, 1, 3, 2, 2)
DY = (0, 1, 0, 0, 1, 1, 0, 1)
F32 = jnp.float32
BF16 = jnp.bfloat16
NT = (((1,), (1,)), ((), ()))


def layer_norm(x, gain, shift):
    mean = jnp.mean(x, axis=-1, keepdims=True)
    center = x - mean
    var = jnp.mean(center * center, axis=-1, keepdims=True)
    return center * lax.rsqrt(var + 1e-05) * gain + shift


def pick(t, table):
    value = jnp.int32(table[0])
    for index in range(1, len(table)):
        value = jnp.where(t == index, jnp.int32(table[index]), value)
    return value


def kernel(
    pair_in,
    mask,
    cid,
    gain,
    shift,
    wp_in,
    gsh,
    bp,
    wo_in,
    ti_in,
    to_in,
    scale,
    out,
    done,
    pair,
    wp,
    wo,
    ti,
    to,
    xs,
    xt,
    xn,
    q,
    k,
    vo,
    gate,
    bt,
    bx,
    gs,
    mrow,
    cidc,
    mz,
    mt,
    mrecv,
    planes,
    stage,
    recv,
    z_send,
    z_recv,
    p_send,
    p_recv,
    f_recv,
    a_send,
    a_recv,
    m_send,
    m_recv,
    l_sem,
    i_sem,
    o_sem,
):
    me = lax.axis_index("dap")
    z = lax.rem(me, NZ)
    pm = lax.div(me, NZ)
    xx = lax.div(pm, 2)
    yy = lax.rem(pm, 2)

    def plane(dx, dy):
        return lax.rem(xx + dx, 4) * 2 + lax.rem(yy + dy, 2)

    def send(src, dst, send_sem, recv_sem, dest):
        pltpu.make_async_remote_copy(
            src_ref=src,
            dst_ref=dst,
            send_sem=send_sem,
            recv_sem=recv_sem,
            device_id={"dap": dest},
            device_id_type=pl.DeviceIdType.MESH,
        ).start()

    def drain(ref, sem):
        pltpu.make_async_copy(ref, ref, sem).wait()

    def fetch(at):
        here = pl.ds(pl.multiple_of(at * 128, 128), 128)
        return pltpu.make_async_copy(
            pair_in.at[:, here, :], pair.at[:, here, :], i_sem.at[at]
        )

    fetched = [
        pltpu.make_async_copy(source, target, i_sem.at[4 + index])
        for index, (source, target) in enumerate(
            ((wp_in, wp), (wo_in, wo), (ti_in, ti), (to_in, to))
        )
    ]
    for at in range(4):
        fetch(at).start()
    for copy in fetched:
        copy.start()
    mz[...] = jnp.zeros_like(mz)
    barrier = pltpu.get_barrier_semaphore()

    def greet(d, carry):
        pl.semaphore_signal(
            barrier,
            inc=1,
            device_id={"dap": lax.rem(me + d, ND)},
            device_id_type=pl.DeviceIdType.MESH,
        )
        return carry

    lax.fori_loop(1, ND, greet, 0)
    mask_f = mask[...].astype(F32)
    mz_at = pl.ds(pl.multiple_of(yy * ROWS + z * 8, 8), 8)
    mz[mz_at, :] = mask_f
    lane_head = lax.div(lax.broadcasted_iota(jnp.int32, (1, 1, C), 2), 32)
    cid_row = cid[...].astype(F32)

    def lanes_of(index):
        return pl.ds(pl.multiple_of(index * 128, 128), 128)

    def norm(layer, at, x):
        xs[layer, :, lanes_of(at), :] = x.reshape(8, 128, C)
        xnv = layer_norm(x, gain[layer : layer + 1, :], shift[layer : layer + 1, :]).astype(BF16)
        xn[at] = xnv
        b = lax.dot_general(bp[layer], xnv, NT, preferred_element_type=F32)
        for r in range(8):
            bt[r * 8 : r * 8 + 4, :] = b[:, r * 128 : (r + 1) * 128]
        own = [bt[pl.ds(h, 8, stride=8), :] for h in range(HEADS)]
        planes[layer, pm, z, at] = jnp.concatenate(own, axis=0).astype(BF16)
        if layer == 0:
            return
        for d in range(1, NZ):
            ref = planes.at[layer, pm, z, at]
            send(ref, ref, z_send.at[layer], z_recv.at[layer, d], pm * NZ + lax.rem(z + d, NZ))
        send(ref, ref, p_send.at[layer], f_recv, plane(2, 0) * NZ + z)

    def project(layer, at):
        f = jnp.dot(xn[at], wp[layer], preferred_element_type=F32)
        here = lanes_of(at)
        q[layer, :, here, :] = (f[:, :C] * (32 ** -0.5)).reshape(8, 128, C)
        k[layer, :, here, :] = f[:, C : 2 * C].astype(BF16).reshape(8, 128, C)
        vo[layer, :, here, :C] = f[:, 2 * C : 3 * C].astype(BF16).reshape(8, 128, C)
        g = jax.nn.sigmoid(f[:, 3 * C :] + gsh[layer : layer + 1, :])
        gate[layer, :, here, :] = g.reshape(8, 128, C)

    def deliver(at):
        here = lanes_of(at)
        return pltpu.make_async_copy(done.at[:, here, :], out.at[:, here, :], o_sem.at[at])

    def arrive(layer, dx):
        source = lax.rem(xx + 4 - dx, 4)
        for yh in range(2):
            m = source * 2 + yh

            @pl.when(m == pm)
            def _():
                drain(recv.at[layer, pl.ds(0, NZ - 1)], a_recv.at[layer, m])

            @pl.when(m != pm)
            def _():
                drain(recv.at[layer, pl.ds(0, NZ)], a_recv.at[layer, m])

        for s in range(16):
            xt[s * 64 : (s + 1) * 64, :] = recv[layer, source * 16 + s].astype(F32)
        columns = [xt[pl.ds(c, 128, stride=8), :] for c in range(8)]
        if layer == 0:
            norm(1, source, jnp.concatenate(columns, axis=0))
        else:
            for i in range(8):
                done[i, lanes_of(source), :] = columns[i].astype(BF16)
            deliver(source).start()

    def first_norm(at, carry):
        fetch(at).wait()
        norm(0, at, pair[:, lanes_of(at), :].astype(F32).reshape(1024, C))
        return carry

    lax.fori_loop(0, 4, first_norm, 0)
    pl.semaphore_wait(barrier, ND - 1)
    def share(ref, layer, m, offsets):
        for dx, dy in offsets:
            send(ref, ref, p_send.at[layer], p_recv.at[layer, m], plane(dx, dy) * NZ + z)

    def share_piece(layer, d):
        source = lax.rem(z + NZ - d, NZ)
        ref = planes.at[layer, pm, source]
        if d:
            drain(ref, z_recv.at[layer, d])
        near = ((0, 1), (1, 0), (3, 0))
        share(ref, layer, pm, near + ((2, 0),) if layer == 0 else near)

    def spread_far(layer):
        far = plane(2, 0)
        ref = planes.at[layer, far, z]
        drain(ref, f_recv)
        for d in (1, 7, 2, 6, 3, 5, 4):
            send(ref, ref, p_send.at[layer], p_recv.at[layer, far], pm * NZ + lax.rem(z + d, NZ))

    for d in (1, 7, 2, 6, 3, 5, 4):
        ref = planes.at[0, pm, z]
        send(ref, ref, z_send.at[0], z_recv.at[0, d], pm * NZ + lax.rem(z + d, NZ))
    share_piece(0, 0)
    for copy in fetched:
        copy.wait()
    project(0, 0)
    share_piece(0, 1)
    share_piece(0, 7)
    project(0, 1)
    share_piece(0, 2)
    share_piece(0, 6)
    project(0, 2)
    share_piece(0, 3)
    share_piece(0, 5)
    project(0, 3)
    cidc[...] = jnp.transpose(jnp.broadcast_to(cid_row, (128, N)))
    mrow[0] = (mask_f - 1.0) * 1e9
    ones = jnp.ones((N, C), BF16)
    for layer in range(2):
        for r in range(8):
            vo[layer, r, :, C:] = ones

    share_piece(0, 4)
    for d in range(1, NZ):
        ref = mz.at[mz_at, :]
        send(ref, ref, m_send.at[0], m_recv.at[0], pm * NZ + lax.rem(z + d, NZ))

    for layer in range(2):
        if layer == 1:
            spread_far(1)
            for d in (0, 1, 7, 2, 6, 3, 5, 4):
                share_piece(1, d)

        def block(t, carry):
            m = plane(pick(t, DX), pick(t, DY))

            @pl.when((t > 0) & (t != 6))
            def _():
                drain(planes.at[layer, m], p_recv.at[layer, m])

            @pl.when(t == 1)
            def _():
                share(planes.at[layer, m], layer, m, ((1, 0), (3, 0)))

            @pl.when(t == 3)
            def _():
                far = plane(2, 0)
                pieces = NZ if layer == 0 else NZ - 1
                drain(planes.at[layer, far, pl.ds(0, pieces)], p_recv.at[layer, far])
                share(planes.at[layer, far], layer, far, ((0, 1),))

            here = pl.ds(pl.multiple_of(m * ROWS, ROWS), ROWS)
            cb = cidc[here, :]
            for c in range(N // 128):
                lanes = slice(c * 128, (c + 1) * 128)
                same = jnp.where(cb == cid_row[:, lanes], 1.0, 0.0).reshape(NZ, 8, 128)
                b = planes[layer, m, :, c].astype(F32).reshape(NZ, HEADS, 8, 128)
                b = jnp.stack(
                    [b[:, h] + scale[layer, h] * same for h in range(HEADS)], axis=1
                )
                bx[:, lanes] = b.reshape(4 * ROWS, 128)

            for i in range(8):
                qi = q[layer, i, here, :].reshape(NZ, 8, C)
                qm = jnp.stack(
                    [jnp.where(lane_head == h, qi, 0.0) for h in range(HEADS)], axis=1
                )
                qm = qm.reshape(4 * ROWS, C).astype(BF16)
                s = lax.dot_general(qm, k[layer, i], NT, preferred_element_type=F32)
                s = s + bx[...] + mrow[layer, i : i + 1, :]
                top = jnp.max(s, axis=-1, keepdims=True)
                p = jnp.exp(s - top).astype(BF16)
                o = jnp.dot(p, vo[layer, i], preferred_element_type=F32)
                o = o.reshape(NZ, HEADS, 8, 2 * C)
                mixed, total = o[:, 0, :, :C], o[:, 0, :, C:]
                for h in range(1, HEADS):
                    mixed = jnp.where(lane_head == h, o[:, h, :, :C], mixed)
                    total = jnp.where(lane_head == h, o[:, h, :, C:], total)
                weighted = (mixed / total).reshape(ROWS, C) * gate[layer, i, here, :]
                gs[i * ROWS : (i + 1) * ROWS, :] = weighted.astype(BF16)

            y = jnp.dot(gs[...], wo[layer], preferred_element_type=F32)
            y = y + xs[layer, :, here, :].reshape(8 * ROWS, C)
            if layer == 1:
                y = y.astype(BF16).astype(F32)
                yn = layer_norm(y, gain[2:3, :], shift[2:3, :]).astype(BF16)
                inner = jnp.dot(yn, ti[...], preferred_element_type=F32)
                inner = jnp.maximum(inner, 0.0).astype(BF16)
                y = y + jnp.dot(inner, to[...], preferred_element_type=F32)
            y = y.reshape(8, NZ, 8, C)
            for zz in range(NZ):
                stage[layer, m, zz] = y[:, zz].reshape(64, C).astype(BF16)

            for d in range(NZ):
                zt = lax.rem(z + d, NZ)

                def go(zt=zt):
                    send(
                        stage.at[layer, m, zt],
                        recv.at[layer, me],
                        a_send.at[layer],
                        a_recv.at[layer, pm],
                        m * NZ + zt,
                    )

                if d == 0:
                    pl.when(t > 0)(go)

                    @pl.when(t == 0)
                    def _():
                        copy = pltpu.make_async_copy(
                            stage.at[layer, m, z], recv.at[layer, me], l_sem
                        )
                        copy.start()
                        copy.wait()
                else:
                    go()

            if layer == 0:

                @pl.when(t == 2)
                def _():
                    drain(mz.at[pl.ds(0, (NZ - 1) * 8)], m_recv.at[0])
                    mt[...] = jnp.transpose(mz[...])
                    for j in range(1, 8):
                        pt = plane(DX[j], DY[j])
                        src = mt.at[pl.ds(pl.multiple_of((pt * NZ + z) * 8, 8), 8), :]
                        send(src, mrecv.at[pm], m_send.at[1], m_recv.at[1], pt * NZ + z)
                    mrecv[pm] = mt[pl.ds(pl.multiple_of(me * 8, 8), 8), :]

            return carry

        lax.fori_loop(0, 8, block, 0)

        def late(index, carry):
            arrive(layer, pick(index, (0, 1, 3, 2)))
            if layer == 0:

                @pl.when(index > 0)
                def _():
                    project(1, lax.rem(xx + 4 - pick(index, (0, 0, 1, 3)), 4))

            return carry

        lax.fori_loop(0, 4, late, 0)
        if layer == 0:
            project(1, lax.rem(xx + 2, 4))
        if layer == 0:
            drain(mrecv.at[pl.ds(0, 7)], m_recv.at[1])
            parts = [mrecv[2 * c] + mrecv[2 * c + 1] for c in range(N // 128)]
            mrow[1] = (jnp.concatenate(parts, axis=1) - 1.0) * 1e9

    for at in range(4):
        deliver(at).wait()
    for layer in range(2):
        drain(planes.at[layer, 0, pl.ds(0, NZ - 1)], z_send.at[layer])
        drain(planes.at[layer, pl.ds(0, 7)], p_send.at[layer])
        drain(recv.at[layer, pl.ds(0, ND - 1)], a_send.at[layer])
    drain(mz.at[pl.ds(0, (NZ - 1) * 8)], m_send.at[0])
    drain(mrecv.at[pl.ds(0, 7)], m_send.at[1])


def body(
    pair,
    pair_mask,
    chain_ids,
    norm_gain,
    norm_shift,
    attn_proj,
    gate_shift,
    bias_proj,
    chain_scale,
    attn_out,
    trans_in,
    trans_out,
):
    vmem = pl.BlockSpec(memory_space=pltpu.VMEM)
    smem = pl.BlockSpec(memory_space=pltpu.SMEM)
    anywhere = pl.BlockSpec(memory_space=pl.ANY)
    dma = pltpu.SemaphoreType.DMA
    return pl.pallas_call(
        kernel,
        out_shape=jax.ShapeDtypeStruct(pair.shape, BF16),
        in_specs=[anywhere] + [vmem] * 4 + [anywhere] + [vmem] * 2 + [anywhere] * 3 + [smem],
        out_specs=anywhere,
        scratch_shapes=[
            pltpu.VMEM((8, N, C), BF16),
            pltpu.VMEM((8, N, C), BF16),
            pltpu.VMEM((2, C, 4 * C), BF16),
            pltpu.VMEM((2, C, C), BF16),
            pltpu.VMEM((C, 4 * C), BF16),
            pltpu.VMEM((4 * C, C), BF16),
            pltpu.VMEM((2, 8, N, C), F32),
            pltpu.VMEM((1024, C), F32),
            pltpu.VMEM((4, 1024, C), BF16),
            pltpu.VMEM((2, 8, N, C), F32),
            pltpu.VMEM((2, 8, N, C), BF16),
            pltpu.VMEM((2, 8, N, 2 * C), BF16),
            pltpu.VMEM((2, 8, N, C), F32),
            pltpu.VMEM((64, 128), F32),
            pltpu.VMEM((4 * ROWS, N), F32),
            pltpu.VMEM((8 * ROWS, C), BF16),
            pltpu.VMEM((2, 8, N), F32),
            pltpu.VMEM((N, 128), F32),
            pltpu.VMEM((128, N), F32),
            pltpu.VMEM((N, 128), F32),
            pltpu.VMEM((8, 8, 128), F32),
            pltpu.VMEM((2, 8, NZ, 4, 32, 128), BF16),
            pltpu.VMEM((2, 8, NZ, 64, C), BF16),
            pltpu.VMEM((2, ND, 64, C), BF16),
            dma((2,)),
            dma((2, NZ)),
            dma((2,)),
            dma((2, 8)),
            dma,
            dma((2,)),
            dma((2, 8)),
            dma((2,)),
            dma((2,)),
            dma,
            dma((8,)),
            dma((4,)),
        ],
        compiler_params=pltpu.CompilerParams(
            collective_id=0,
            has_side_effects=True,
            vmem_limit_bytes=56 * 1024 * 1024,
        ),
    )(
        pair,
        pair_mask,
        chain_ids.reshape(1, N),
        norm_gain,
        norm_shift,
        attn_proj,
        gate_shift,
        jnp.swapaxes(bias_proj, 1, 2),
        attn_out,
        trans_in,
        trans_out,
        chain_scale,
    )


def solution(mesh):
    in_specs = (
        P(("rep", "dap"), None, None),
        P(("rep", "dap"), None),
        P("rep"),
    ) + (P(),) * 9
    out_specs = P(("rep", "dap"), None, None)
    return jax.shard_map(body, mesh=mesh, in_specs=in_specs, out_specs=out_specs, check_vma=False)
```

```python
import functools

import jax
import jax.numpy as jnp
from jax import lax
from jax.experimental import pallas as pl
from jax.experimental.pallas import tpu as pltpu
from jax.sharding import PartitionSpec as P

C = 128
HEADS = 4
NZ = 8
ND = 64
N = 512
ROWS = 64
DX = (0, 0, 1, 3, 1, 3, 2, 2)
DY = (0, 1, 0, 0, 1, 1, 0, 1)
F32 = jnp.float32
BF16 = jnp.bfloat16
NT = (((1,), (1,)), ((), ()))


def layer_norm(x, gain, shift):
    mean = jnp.mean(x, axis=-1, keepdims=True)
    center = x - mean
    var = jnp.mean(center * center, axis=-1, keepdims=True)
    return center * lax.rsqrt(var + 1e-05) * gain + shift


def pick(t, table):
    value = jnp.int32(table[0])
    for index in range(1, len(table)):
        value = jnp.where(t == index, jnp.int32(table[index]), value)
    return value


def kernel(
    pair_in,
    mask,
    cid,
    gain,
    shift,
    wp_in,
    gsh,
    bp,
    wo_in,
    ti_in,
    to_in,
    scale,
    out,
    done,
    pair,
    wp,
    wo,
    ti,
    to,
    xs,
    xt,
    xn,
    q,
    k,
    vo,
    gate,
    bt,
    bx,
    gs,
    mrow,
    cidc,
    mz,
    mt,
    mrecv,
    planes,
    stage,
    recv,
    z_send,
    z_recv,
    p_send,
    p_recv,
    f_recv,
    a_send,
    a_recv,
    m_send,
    m_recv,
    l_sem,
    i_sem,
    o_sem,
):
    me = lax.axis_index("dap")
    z = lax.rem(me, NZ)
    pm = lax.div(me, NZ)
    xx = lax.div(pm, 2)
    yy = lax.rem(pm, 2)

    def plane(dx, dy):
        return lax.rem(xx + dx, 4) * 2 + lax.rem(yy + dy, 2)

    def send(src, dst, send_sem, recv_sem, dest):
        pltpu.make_async_remote_copy(
            src_ref=src,
            dst_ref=dst,
            send_sem=send_sem,
            recv_sem=recv_sem,
            device_id={"dap": dest},
            device_id_type=pl.DeviceIdType.MESH,
        ).start()

    def drain(ref, sem):
        pltpu.make_async_copy(ref, ref, sem).wait()

    def fetch(at):
        here = pl.ds(pl.multiple_of(at * 128, 128), 128)
        return pltpu.make_async_copy(
            pair_in.at[:, here, :], pair.at[:, here, :], i_sem.at[at]
        )

    fetched = [
        pltpu.make_async_copy(source, target, i_sem.at[4 + index])
        for index, (source, target) in enumerate(
            ((wp_in, wp), (wo_in, wo), (ti_in, ti), (to_in, to))
        )
    ]
    for at in range(4):
        fetch(at).start()
    for copy in fetched:
        copy.start()
    mz[...] = jnp.zeros_like(mz)
    barrier = pltpu.get_barrier_semaphore()

    def greet(d, carry):
        pl.semaphore_signal(
            barrier,
            inc=1,
            device_id={"dap": lax.rem(me + d, ND)},
            device_id_type=pl.DeviceIdType.MESH,
        )
        return carry

    lax.fori_loop(1, ND, greet, 0)
    mask_f = mask[...].astype(F32)
    mz_at = pl.ds(pl.multiple_of(yy * ROWS + z * 8, 8), 8)
    mz[mz_at, :] = mask_f
    lane_head = lax.div(lax.broadcasted_iota(jnp.int32, (1, 1, C), 2), 32)
    cid_row = cid[...].astype(F32)

    def lanes_of(index):
        return pl.ds(pl.multiple_of(index * 128, 128), 128)

    def norm(layer, at, x):
        xs[layer, :, lanes_of(at), :] = x.reshape(8, 128, C)
        xnv = layer_norm(x, gain[layer : layer + 1, :], shift[layer : layer + 1, :]).astype(BF16)
        xn[at] = xnv
        b = lax.dot_general(bp[layer], xnv, NT, preferred_element_type=F32)
        for r in range(8):
            bt[r * 8 : r * 8 + 4, :] = b[:, r * 128 : (r + 1) * 128]
        own = [bt[pl.ds(h, 8, stride=8), :] for h in range(HEADS)]
        planes[layer, pm, z, at] = jnp.concatenate(own, axis=0).astype(BF16)
        if layer == 0:
            return
        for d in range(1, NZ):
            ref = planes.at[layer, pm, z, at]
            send(ref, ref, z_send.at[layer], z_recv.at[layer, d], pm * NZ + lax.rem(z + d, NZ))
        send(ref, ref, p_send.at[layer], f_recv, plane(2, 0) * NZ + z)

    def project(layer, at):
        f = jnp.dot(xn[at], wp[layer], preferred_element_type=F32)
        here = lanes_of(at)
        q[layer, :, here, :] = (f[:, :C] * (32 ** -0.5)).reshape(8, 128, C)
        k[layer, :, here, :] = f[:, C : 2 * C].astype(BF16).reshape(8, 128, C)
        vo[layer, :, here, :C] = f[:, 2 * C : 3 * C].astype(BF16).reshape(8, 128, C)
        g = jax.nn.sigmoid(f[:, 3 * C :] + gsh[layer : layer + 1, :])
        gate[layer, :, here, :] = g.reshape(8, 128, C)

    def deliver(at):
        here = lanes_of(at)
        return pltpu.make_async_copy(done.at[:, here, :], out.at[:, here, :], o_sem.at[at])

    def arrive(layer, dx):
        source = lax.rem(xx + 4 - dx, 4)
        for yh in range(2):
            m = source * 2 + yh

            @pl.when(m == pm)
            def _():
                drain(recv.at[layer, pl.ds(0, NZ - 1)], a_recv.at[layer, m])

            @pl.when(m != pm)
            def _():
                drain(recv.at[layer, pl.ds(0, NZ)], a_recv.at[layer, m])

        for s in range(16):
            xt[s * 64 : (s + 1) * 64, :] = recv[layer, source * 16 + s].astype(F32)
        columns = [xt[pl.ds(c, 128, stride=8), :] for c in range(8)]
        if layer == 0:
            norm(1, source, jnp.concatenate(columns, axis=0))
        else:
            for i in range(8):
                done[i, lanes_of(source), :] = columns[i].astype(BF16)
            deliver(source).start()

    def first_norm(at, carry):
        fetch(at).wait()
        norm(0, at, pair[:, lanes_of(at), :].astype(F32).reshape(1024, C))
        return carry

    lax.fori_loop(0, 4, first_norm, 0)
    pl.semaphore_wait(barrier, ND - 1)
    def share(ref, layer, m, offsets):
        for dx, dy in offsets:
            send(ref, ref, p_send.at[layer], p_recv.at[layer, m], plane(dx, dy) * NZ + z)

    def share_piece(layer, d):
        source = lax.rem(z + NZ - d, NZ)
        ref = planes.at[layer, pm, source]
        if d:
            drain(ref, z_recv.at[layer, d])
        near = ((0, 1), (1, 0), (3, 0))
        share(ref, layer, pm, near + ((2, 0),) if layer == 0 else near)

    def spread_far(layer):
        far = plane(2, 0)
        ref = planes.at[layer, far, z]
        drain(ref, f_recv)
        for d in (1, 7, 2, 6, 3, 5, 4):
            send(ref, ref, p_send.at[layer], p_recv.at[layer, far], pm * NZ + lax.rem(z + d, NZ))

    for d in (1, 7, 2, 6, 3, 5, 4):
        ref = planes.at[0, pm, z]
        send(ref, ref, z_send.at[0], z_recv.at[0, d], pm * NZ + lax.rem(z + d, NZ))
    share_piece(0, 0)
    for copy in fetched:
        copy.wait()
    project(0, 0)
    share_piece(0, 1)
    share_piece(0, 7)
    project(0, 1)
    share_piece(0, 2)
    share_piece(0, 6)
    project(0, 2)
    share_piece(0, 3)
    share_piece(0, 5)
    project(0, 3)
    cidc[...] = jnp.transpose(jnp.broadcast_to(cid_row, (128, N)))
    mrow[0] = (mask_f - 1.0) * 1e9
    ones = jnp.ones((N, C), BF16)
    for layer in range(2):
        for r in range(8):
            vo[layer, r, :, C:] = ones

    share_piece(0, 4)
    for d in range(1, NZ):
        ref = mz.at[mz_at, :]
        send(ref, ref, m_send.at[0], m_recv.at[0], pm * NZ + lax.rem(z + d, NZ))

    for layer in range(2):
        if layer == 1:
            spread_far(1)
            for d in (0, 1, 7, 2, 6, 3, 5, 4):
                share_piece(1, d)

        def block(t, carry):
            m = plane(pick(t, DX), pick(t, DY))

            @pl.when((t > 0) & (t != 6))
            def _():
                drain(planes.at[layer, m], p_recv.at[layer, m])

            @pl.when(t == 1)
            def _():
                share(planes.at[layer, m], layer, m, ((1, 0), (3, 0)))

            @pl.when(t == 3)
            def _():
                far = plane(2, 0)
                pieces = NZ if layer == 0 else NZ - 1
                drain(planes.at[layer, far, pl.ds(0, pieces)], p_recv.at[layer, far])
                share(planes.at[layer, far], layer, far, ((0, 1),))

            here = pl.ds(pl.multiple_of(m * ROWS, ROWS), ROWS)
            cb = cidc[here, :]
            for c in range(N // 128):
                lanes = slice(c * 128, (c + 1) * 128)
                same = jnp.where(cb == cid_row[:, lanes], 1.0, 0.0).reshape(NZ, 8, 128)
                b = planes[layer, m, :, c].astype(F32).reshape(NZ, HEADS, 8, 128)
                b = jnp.stack(
                    [b[:, h] + scale[layer, h] * same for h in range(HEADS)], axis=1
                )
                bx[:, lanes] = b.reshape(4 * ROWS, 128)

            for i in range(8):
                qi = q[layer, i, here, :].reshape(NZ, 8, C)
                qm = jnp.stack(
                    [jnp.where(lane_head == h, qi, 0.0) for h in range(HEADS)], axis=1
                )
                qm = qm.reshape(4 * ROWS, C).astype(BF16)
                s = lax.dot_general(qm, k[layer, i], NT, preferred_element_type=F32)
                s = s + bx[...] + mrow[layer, i : i + 1, :]
                top = jnp.max(s, axis=-1, keepdims=True)
                p = jnp.exp(s - top).astype(BF16)
                o = jnp.dot(p, vo[layer, i], preferred_element_type=F32)
                o = o.reshape(NZ, HEADS, 8, 2 * C)
                mixed, total = o[:, 0, :, :C], o[:, 0, :, C:]
                for h in range(1, HEADS):
                    mixed = jnp.where(lane_head == h, o[:, h, :, :C], mixed)
                    total = jnp.where(lane_head == h, o[:, h, :, C:], total)
                weighted = (mixed / total).reshape(ROWS, C) * gate[layer, i, here, :]
                gs[i * ROWS : (i + 1) * ROWS, :] = weighted.astype(BF16)

            y = jnp.dot(gs[...], wo[layer], preferred_element_type=F32)
            y = y + xs[layer, :, here, :].reshape(8 * ROWS, C)
            if layer == 1:
                y = y.astype(BF16).astype(F32)
                yn = layer_norm(y, gain[2:3, :], shift[2:3, :]).astype(BF16)
                inner = jnp.dot(yn, ti[...], preferred_element_type=F32)
                inner = jnp.maximum(inner, 0.0).astype(BF16)
                y = y + jnp.dot(inner, to[...], preferred_element_type=F32)
            y = y.reshape(8, NZ, 8, C)
            for zz in range(NZ):
                stage[layer, m, zz] = y[:, zz].reshape(64, C).astype(BF16)

            for d in range(NZ):
                zt = lax.rem(z + (0, 4, 3, 5, 2, 6, 1, 7)[d], NZ)

                def go(zt=zt):
                    send(
                        stage.at[layer, m, zt],
                        recv.at[layer, me],
                        a_send.at[layer],
                        a_recv.at[layer, pm],
                        m * NZ + zt,
                    )

                if d == 0:
                    pl.when(t > 0)(go)

                    @pl.when(t == 0)
                    def _():
                        copy = pltpu.make_async_copy(
                            stage.at[layer, m, z], recv.at[layer, me], l_sem
                        )
                        copy.start()
                        copy.wait()
                else:
                    go()

            if layer == 0:

                @pl.when(t == 2)
                def _():
                    drain(mz.at[pl.ds(0, (NZ - 1) * 8)], m_recv.at[0])
                    mt[...] = jnp.transpose(mz[...])
                    for j in range(1, 8):
                        pt = plane(DX[j], DY[j])
                        src = mt.at[pl.ds(pl.multiple_of((pt * NZ + z) * 8, 8), 8), :]
                        send(src, mrecv.at[pm], m_send.at[1], m_recv.at[1], pt * NZ + z)
                    mrecv[pm] = mt[pl.ds(pl.multiple_of(me * 8, 8), 8), :]

            return carry

        lax.fori_loop(0, 8, block, 0)

        def late(index, carry):
            arrive(layer, pick(index, (0, 1, 3, 2)))
            if layer == 0:

                @pl.when(index > 0)
                def _():
                    project(1, lax.rem(xx + 4 - pick(index, (0, 0, 1, 3)), 4))

            return carry

        lax.fori_loop(0, 4, late, 0)
        if layer == 0:
            project(1, lax.rem(xx + 2, 4))
        if layer == 0:
            drain(mrecv.at[pl.ds(0, 7)], m_recv.at[1])
            parts = [mrecv[2 * c] + mrecv[2 * c + 1] for c in range(N // 128)]
            mrow[1] = (jnp.concatenate(parts, axis=1) - 1.0) * 1e9

    for at in range(4):
        deliver(at).wait()
    for layer in range(2):
        drain(planes.at[layer, 0, pl.ds(0, NZ - 1)], z_send.at[layer])
        drain(planes.at[layer, pl.ds(0, 7)], p_send.at[layer])
        drain(recv.at[layer, pl.ds(0, ND - 1)], a_send.at[layer])
    drain(mz.at[pl.ds(0, (NZ - 1) * 8)], m_send.at[0])
    drain(mrecv.at[pl.ds(0, 7)], m_send.at[1])


def body(
    pair,
    pair_mask,
    chain_ids,
    norm_gain,
    norm_shift,
    attn_proj,
    gate_shift,
    bias_proj,
    chain_scale,
    attn_out,
    trans_in,
    trans_out,
):
    vmem = pl.BlockSpec(memory_space=pltpu.VMEM)
    smem = pl.BlockSpec(memory_space=pltpu.SMEM)
    anywhere = pl.BlockSpec(memory_space=pl.ANY)
    dma = pltpu.SemaphoreType.DMA
    return pl.pallas_call(
        kernel,
        out_shape=jax.ShapeDtypeStruct(pair.shape, BF16),
        in_specs=[anywhere] + [vmem] * 4 + [anywhere] + [vmem] * 2 + [anywhere] * 3 + [smem],
        out_specs=anywhere,
        scratch_shapes=[
            pltpu.VMEM((8, N, C), BF16),
            pltpu.VMEM((8, N, C), BF16),
            pltpu.VMEM((2, C, 4 * C), BF16),
            pltpu.VMEM((2, C, C), BF16),
            pltpu.VMEM((C, 4 * C), BF16),
            pltpu.VMEM((4 * C, C), BF16),
            pltpu.VMEM((2, 8, N, C), F32),
            pltpu.VMEM((1024, C), F32),
            pltpu.VMEM((4, 1024, C), BF16),
            pltpu.VMEM((2, 8, N, C), F32),
            pltpu.VMEM((2, 8, N, C), BF16),
            pltpu.VMEM((2, 8, N, 2 * C), BF16),
            pltpu.VMEM((2, 8, N, C), F32),
            pltpu.VMEM((64, 128), F32),
            pltpu.VMEM((4 * ROWS, N), F32),
            pltpu.VMEM((8 * ROWS, C), BF16),
            pltpu.VMEM((2, 8, N), F32),
            pltpu.VMEM((N, 128), F32),
            pltpu.VMEM((128, N), F32),
            pltpu.VMEM((N, 128), F32),
            pltpu.VMEM((8, 8, 128), F32),
            pltpu.VMEM((2, 8, NZ, 4, 32, 128), BF16),
            pltpu.VMEM((2, 8, NZ, 64, C), BF16),
            pltpu.VMEM((2, ND, 64, C), BF16),
            dma((2,)),
            dma((2, NZ)),
            dma((2,)),
            dma((2, 8)),
            dma,
            dma((2,)),
            dma((2, 8)),
            dma((2,)),
            dma((2,)),
            dma,
            dma((8,)),
            dma((4,)),
        ],
        compiler_params=pltpu.CompilerParams(
            collective_id=0,
            has_side_effects=True,
            vmem_limit_bytes=56 * 1024 * 1024,
        ),
    )(
        pair,
        pair_mask,
        chain_ids.reshape(1, N),
        norm_gain,
        norm_shift,
        attn_proj,
        gate_shift,
        jnp.swapaxes(bias_proj, 1, 2),
        attn_out,
        trans_in,
        trans_out,
        chain_scale,
    )


def solution(mesh):
    in_specs = (
        P(("rep", "dap"), None, None),
        P(("rep", "dap"), None),
        P("rep"),
    ) + (P(),) * 9
    out_specs = P(("rep", "dap"), None, None)
    return jax.shard_map(body, mesh=mesh, in_specs=in_specs, out_specs=out_specs, check_vma=False)
```
